32 devices in a mesh: parts: 2 (over x), tp: 16 (over z, y, core).
Axes of the slice: x: 2, y: 2, z: 4, core: 2. Of those that a mesh axis runs over, the one named last changes fastest.
Arguments:
- tokens: bfloat16 [2048, 3072], P(('parts', 'tp')), parts along dimension 0, may hold values from -6 to 6
- routes: int32 [2048, 2], P(('parts', 'tp')), parts along dimension 0, may hold values from 0 to 7, all different within a row; in each aligned block of 64 rows (0 to 63, 64 to 127, ...) at most 18 rows name the same one
- gates: float32 [2048, 2], P(('parts', 'tp')), parts along dimension 0, may hold values from 0.25 to 1
- w_gate: bfloat16 [3072, 43008], P(None, 'tp'), may hold values from -0.109375 to 0.109375
- w_up: bfloat16 [3072, 43008], P(None, 'tp'), may hold values from -0.109375 to 0.109375
- w_down: bfloat16 [43008, 3072], P('tp'), may hold values from -0.078125 to 0.078125
Outputs:
- moe_out: bfloat16 [2048, 3072], P(('parts', 'tp')), parts along dimension 0
The draws below stay inside these ranges and needn't reach their ends.
There are 2 independent parts, one for each index of `parts`. The reference program is written for one: setup_inputs(seed, part) draws one part's arguments, and reference() takes and returns one part's arrays. A program takes and returns all parts, laid end to end along the dimension named above; an argument that names none is the same for every part. Nothing has to cross between parts.
Inputs may be any that keep to these rules, and one draw needn't show every extreme that they name: `routes`: each token names 2 different experts. Within the rows of one device no expert is named more than 18 times, and in the rows of some device one expert is named exactly 18 times.
All inputs are finite; a program needn't handle non-finite values.
Results may differ from the reference program's by a relative error of at most 0.0058.
Values may be sent and summed in bfloat16 or wider, within the bound.
A program may use at most 192 MiB of HBM per device.

```python
import math
import jax
import jax.numpy as jnp
import numpy as np
from jax import lax

D = 3072
FF = 5376
EXPERTS = 8
TOP = 2
TOK_DEV = 64
TOKENS = 1024
CYCLE = 2
CAP = 18
N_TP = 16


def block_scale(rng, extent, pieces, low, high):
    def one(dim, shards_of):
        steps = jax.random.uniform(jax.random.fold_in(jax.random.fold_in(rng, 6), dim), (shards_of,), jnp.float32, low / len(pieces), high / len(pieces))
        return jnp.repeat(jnp.exp(steps), extent[dim] // shards_of).reshape((-1,) + (1,) * (len(extent) - dim - 1))

    level = one(*pieces[0])
    for cut in pieces[1:]:
        level = level * one(*cut)
    return level


def deal_out(stream_key, own, number, rows, count, top, reach, lean):
    ranking = jax.random.permutation(stream_key, count)
    heavy_load, common = portions_of(count, rows * top, reach, lean, True), portions_of(count, rows * top, reach, lean, False)
    places = jnp.arange(count)

    def named(tallies, turn):
        used = int((tallies > 0).sum())
        fixed = max(1, used // 4)
        passed = fixed + (places - fixed + turn * (used - fixed)) % max(1, count - fixed)
        return jnp.zeros((count,), jnp.int32).at[ranking[jnp.where(places < fixed, places, passed)]].set(jnp.asarray(tallies, jnp.int32))

    tallies = jnp.where(number % 4 == 0, named(heavy_load, number // 4), named(common, number - number // 4 - 1))
    mixed = jax.random.permutation(jax.random.fold_in(own, 3), count)
    source_of, sink = mixed[0:count // 2 * 2:2], mixed[1:count // 2 * 2:2]
    margin = jnp.minimum(tallies[source_of] - 1, reach - tallies[sink]) // 2
    margin = jnp.where((source_of == ranking[0]) | (sink == ranking[0]) | (tallies[sink] == 0), 0, jnp.maximum(margin, 0))
    passed = jax.random.randint(jax.random.fold_in(own, 4), (count // 2,), 0, 1 << 20) % (margin + 1)
    tallies = tallies.at[source_of].add(-passed).at[sink].add(passed)
    labels = jnp.searchsorted(jnp.cumsum(tallies), jnp.arange(rows * top), side="right").astype(jnp.int32)
    table = labels.reshape(top, rows).T
    table = table[jax.random.permutation(jax.random.fold_in(own, 1), rows)]
    turn = jax.random.randint(jax.random.fold_in(own, 2), (rows, 1), 0, top)
    return jnp.take_along_axis(table, (jnp.arange(top)[None, :] + turn) % top, axis=1)


def portions_of(number_of, total, limit, skew, full):
    portions = [(1 << 20) // math.isqrt(standing ** skew) + 1 for standing in range(1, number_of + 1)]
    largest = limit if full else min(limit, max(-(-total // number_of), total * portions[0] // sum(portions)))
    least = 1 if total - largest >= number_of - 1 else 0
    counts, surplus = [largest] + [least] * (number_of - 1), total - largest - least * (number_of - 1)
    while surplus > 0:
        free = [i for i in range(1, number_of) if counts[i] < largest] or [i for i in range(1, number_of) if counts[i] < limit]
        mass, remaining = sum([portions[i] for i in free]), surplus
        for i in free:
            extra = min(limit - counts[i], max(1, remaining * portions[i] // mass), surplus)
            counts[i] = counts[i] + extra
            surplus = surplus - extra
    return np.array(counts)


def gaussian(rng, shape, deviation, reach, shards=(), kind=jnp.bfloat16):
    array = deviation * jax.random.normal(rng, shape, jnp.float32)
    if shards:
        array = array * block_scale(rng, shape, shards, -0.22, 0.18)
    return jnp.clip(array, -reach, reach).astype(kind)


def setup_inputs(seed: int = 0, part: int = 0) -> dict:
    seeds = jax.random.split(jax.random.key(seed), 7)
    part_keys = jax.random.split(jax.random.fold_in(seeds[6], part), 7)
    tokens = gaussian(part_keys[0], (TOKENS, D), 1.0, 6.0, ((0, 16),))
    routes_keys = jax.random.split(jax.random.fold_in(part_keys[1], 1), TOKENS // TOK_DEV)
    routes_turns = jax.random.permutation(jax.random.fold_in(part_keys[1], 3), TOKENS // TOK_DEV)
    routes = jax.vmap(lambda own, number: deal_out(jax.random.fold_in(part_keys[1], 2), own, number, TOK_DEV, EXPERTS, TOP, CAP, 2))(routes_keys, routes_turns).reshape((TOKENS, TOP))
    gates = jnp.clip(0.25 + 0.75 * jax.random.uniform(part_keys[2], (TOKENS, TOP), jnp.float32) ** block_scale(part_keys[2], (TOKENS, TOP), ((0, 16),), -0.2, 0.2), 0.25, 1.0)
    w_gate = gaussian(seeds[3], (D, EXPERTS * FF), D ** -0.5, 0.109375, ((1, 16),))
    w_up = gaussian(seeds[4], (D, EXPERTS * FF), D ** -0.5, 0.109375, ((1, 16),))
    w_down = gaussian(seeds[5], (EXPERTS * FF, D), FF ** -0.5, 0.078125, ((0, 16),))
    return dict(tokens=tokens, routes=routes, gates=gates, w_gate=w_gate, w_up=w_up, w_down=w_down)


def reference(tokens, routes, gates, w_gate, w_up, w_down):
    routed = routes.reshape(-1).astype(jnp.int32)
    pair_count = routed.shape[0]
    gate_cube = w_gate.reshape(D, EXPERTS, FF)
    up_cube = w_up.reshape(D, EXPERTS, FF)
    down_cube = w_down.reshape(EXPERTS, FF, D)
    capacity = N_TP * CAP
    block_width = FF // CYCLE

    def one_expert(expert):
        chosen = jnp.nonzero(routed == expert, size=capacity, fill_value=pair_count)[0].astype(jnp.int32)
        source_tok = jnp.where(chosen < pair_count, chosen // TOP, 0).astype(jnp.int32)
        gathered_rows = tokens[source_tok]
        gate_act = jnp.dot(gathered_rows, lax.dynamic_index_in_dim(gate_cube, expert, 1, keepdims=False), preferred_element_type=jnp.float32)
        up_act = jnp.dot(gathered_rows, lax.dynamic_index_in_dim(up_cube, expert, 1, keepdims=False), preferred_element_type=jnp.float32)
        hidden = (jax.nn.silu(gate_act) * up_act).astype(jnp.bfloat16)
        down_mat = lax.dynamic_index_in_dim(down_cube, expert, 0, keepdims=False)

        def add_block(block, total):
            start = (block * block_width).astype(jnp.int32)
            hid_part = lax.dynamic_slice_in_dim(hidden, start, block_width, 1)
            down_part = lax.dynamic_slice_in_dim(down_mat, start, block_width, 0)
            piece = jnp.dot(hid_part, down_part, preferred_element_type=jnp.float32).astype(jnp.bfloat16)
            piece = lax.optimization_barrier(piece)
            return total + piece.astype(jnp.float32)

        result = lax.fori_loop(0, CYCLE, add_block, jnp.zeros((capacity, D), jnp.float32))
        return result, chosen

    expert_rows, places = lax.map(one_expert, jnp.arange(EXPERTS, dtype=jnp.int32))
    assigned = jnp.zeros((pair_count, D), jnp.float32).at[places.reshape(-1)].add(expert_rows.reshape(-1, D), mode="drop")
    weighted = assigned.reshape(TOKENS, TOP, D) * gates[:, :, None]
    return jnp.sum(weighted, axis=1).astype(jnp.bfloat16)
```

```python
import functools

import jax
import jax.numpy as jnp
from jax import lax
from jax.experimental import pallas as pl
from jax.experimental.pallas import tpu as pltpu
from jax.sharding import PartitionSpec as P

EXPERTS = 8
TOP = 2
CAP = 18
BASE = 16
MESH = pl.DeviceIdType.MESH
BF = jnp.bfloat16
F32 = jnp.float32


def swapped(x, axis, bit):
    return lax.ppermute(x, axis, [(i, i ^ 1 << bit) for i in range(lax.axis_size(axis))])


def passed_along(value, axis, steps):
    count = lax.axis_size(axis)
    pairs = [(source, (source + steps) % count) for source in range(count)]
    return lax.ppermute(value, axis, pairs)


def expert_rows(chosen_rows, w_gate, w_up, w_down):
    gate_act = jnp.dot(chosen_rows, w_gate, preferred_element_type=jnp.float32)
    up_act = jnp.dot(chosen_rows, w_up, preferred_element_type=jnp.float32)
    hidden = (jax.nn.silu(gate_act) * up_act).astype(jnp.bfloat16)
    return jnp.dot(hidden, w_down, preferred_element_type=jnp.float32)


def local_any(tokens, routes, gates, w_gate, w_up, w_down):
    devices = lax.axis_size("tp")
    cycle_size = devices // EXPERTS
    levels = cycle_size.bit_length() - 1
    my_index = lax.axis_index("tp")
    my_group = my_index // cycle_size
    tok_count, feat_width = tokens.shape
    routed = routes.reshape(-1)
    pair_count = routed.shape[0]
    onehot = (routed[:, None] == jnp.arange(EXPERTS, dtype=jnp.int32)[None, :]).astype(jnp.int32)
    before = jnp.cumsum(onehot, axis=0) - onehot
    slot_index = jnp.sum(before * onehot, axis=1)
    target = routed * CAP + slot_index
    source_tok = jnp.arange(pair_count, dtype=jnp.int32) // TOP
    outgoing = (
        jnp.zeros((EXPERTS * CAP, feat_width), jnp.bfloat16).at[target].set(tokens[source_tok])
    )
    outgoing = outgoing.reshape(EXPERTS, CAP, feat_width)
    group_order = (my_group - jnp.arange(EXPERTS, dtype=jnp.int32)) % EXPERTS
    spread = jnp.repeat(outgoing, cycle_size, axis=0)
    incoming = lax.all_to_all(spread, "tp", split_axis=0, concat_axis=0, tiled=True)
    flat_rows = incoming.reshape(devices * CAP, feat_width)
    partial_value = expert_rows(flat_rows, w_gate, w_up, w_down)
    partial_value = partial_value.astype(jnp.bfloat16).reshape(devices, CAP, feat_width)
    current = lax.optimization_barrier(partial_value).astype(jnp.float32)
    current = current.reshape(EXPERTS, cycle_size, CAP, feat_width)
    for bit in range(levels):
        halves = current.reshape(EXPERTS, current.shape[1] // 2, 2, CAP, feat_width)
        upper = my_index // (1 << bit) % 2 == 1
        kept = jnp.where(upper, halves[:, :, 1], halves[:, :, 0])
        sending = jnp.where(upper, halves[:, :, 0], halves[:, :, 1])
        current = kept + swapped(sending.astype(jnp.bfloat16), "tp", bit).astype(sending.dtype)
    owned = current.reshape(EXPERTS, CAP, feat_width)
    back = [lax.dynamic_index_in_dim(owned, my_group, 0, keepdims=False)]
    for offset in range(1, EXPERTS):
        chosen = lax.dynamic_index_in_dim(owned, (my_group + offset) % EXPERTS, 0, keepdims=False)
        back.append(passed_along(chosen, "tp", offset * cycle_size))
    expert_out = jnp.take(jnp.stack(back), group_order, axis=0)
    picked = expert_out.reshape(EXPERTS * CAP, feat_width)[target]
    weighted = picked.reshape(tok_count, TOP, feat_width) * gates[:, :, None]
    return jnp.sum(weighted, axis=1).astype(jnp.bfloat16)


PARTS = 3
NT = 7


def iota(shape, dim):
    return lax.broadcasted_iota(jnp.int32, shape, dim)


def kernel(
    tok, routes, gates, wg, wu, wd, out,
    w_in, w_out, acc, hid, x, send, recv_a, recv_b, own, part_s, part_r, rsend, ret, gsc,
    in_sem, out_sem, ssem, rsem, fs_sem, fr_sem, ps_sem, pr_sem, bs_sem, br_sem,
):
    n_tok, feat = tok.shape
    kc = feat // PARTS
    ow = kc // 8
    ff = wg.shape[1]
    tw = ff // NT
    rows = EXPERTS * BASE
    ext = EXPERTS * 2
    half = rows + ext
    me = lax.axis_index("tp")
    group = lax.div(me, 2)
    core = lax.rem(me, 2)
    twin = {"tp": group * 2 + (1 - core)}

    def peer(d):
        return lax.rem(group + d, EXPERTS)

    def in_copies(c):
        res = []
        for j in range(NT):
            for s, w in enumerate((wg, wu)):
                res.append(pltpu.make_async_copy(
                    w.at[pl.ds(c * kc, kc), pl.ds(j * tw, tw)],
                    w_in.at[c, :, pl.ds((2 * j + s) * tw, tw)],
                    in_sem.at[c, 2 * j + s]))
        return res

    def out_copy(n):
        return pltpu.make_async_copy(
            wd.at[:, pl.ds(n * kc, kc)], w_out.at[n % 2], out_sem.at[n % 2])

    barrier = pltpu.get_barrier_semaphore()
    for d in range(1, EXPERTS):
        pl.semaphore_signal(barrier, inc=1, device_id={"tp": peer(d) * 2 + core}, device_id_type=MESH)
    pl.semaphore_signal(barrier, inc=1, device_id=twin, device_id_type=MESH)
    for c in range(PARTS):
        for cp in in_copies(c):
            cp.start()
    for n in range(2):
        out_copy(n).start()

    lane = iota((n_tok, rows), 1)
    lane_group = lane >> 4
    place = lane & 15
    first = routes[:, 0:1] == lane_group
    second = routes[:, 1:2] == lane_group
    named = jnp.where(first | second, 1.0, 0.0).astype(F32)
    gate = jnp.where(first, gates[:, 0:1], 0.0) + jnp.where(second, gates[:, 1:2], 0.0)
    earlier = jnp.where(iota((n_tok, n_tok), 1) < iota((n_tok, n_tok), 0), 1.0, 0.0).astype(BF)
    slot = jnp.dot(earlier, named.astype(BF), preferred_element_type=F32).astype(jnp.int32)
    main = jnp.where(slot == place, named, 0.0)
    over = jnp.where(slot == BASE + (place >> 3), named, 0.0)
    overs = jnp.concatenate(
        [jnp.where((lane & 7) == k, over, 0.0) for k in range(8)], axis=0)
    flipped = jnp.concatenate([overs, main, jnp.zeros_like(main)], axis=0).T.astype(BF)
    over_t, main_t = flipped[:, :8 * n_tok], flipped[:, 8 * n_tok:9 * n_tok]
    full = jnp.concatenate([overs * jnp.concatenate([gate] * 8, axis=0), main * gate], axis=0)
    high = full.astype(BF)
    gsc[0] = high
    gsc[1] = (full - high.astype(F32)).astype(BF)

    i, j = iota((rows, rows), 0), iota((rows, rows), 1)
    unpack = ((i >> 4) == (j & 7)) & (((i & 15) >> 1) == (j >> 4)) & ((i & 1) == ((j & 15) >> 3))
    unpack = jnp.where(unpack, 1.0, 0.0).astype(BF)
    pack = ((j >> 4) == (i & 7)) & (((j & 15) >> 1) == (i >> 4)) & ((j & 1) == ((i & 15) >> 3))
    pack = jnp.where(pack, 1.0, 0.0).astype(BF)

    def block(g):
        return pl.ds(pl.multiple_of(g * BASE, BASE), BASE)

    def ship(src, dst, s_sem, r_sem, c, d):
        to = peer(d)
        return pltpu.make_async_remote_copy(
            src_ref=src.at[c, block(to)], dst_ref=dst.at[c, block(group)],
            send_sem=s_sem.at[c, d], recv_sem=r_sem.at[c, group],
            device_id={"tp": to * 2 + core}, device_id_type=MESH)

    def landed(dst, s_sem, r_sem, c, d):
        src = lax.rem(group + EXPERTS - d, EXPERTS)
        return pltpu.make_async_remote_copy(
            src_ref=dst.at[c, block(src)], dst_ref=dst.at[c, block(src)],
            send_sem=s_sem.at[c, d], recv_sem=r_sem.at[c, src],
            device_id=twin, device_id_type=MESH)

    for c in range(PARTS):
        cols = tok[:, c * kc:(c + 1) * kc]
        send[c, :, :kc] = jnp.dot(main_t, cols, preferred_element_type=F32).astype(BF)
        tall = jnp.concatenate([cols[:, k * ow:(k + 1) * ow] for k in range(8)], axis=0)
        send[c, :, kc:] = jnp.dot(over_t, tall, preferred_element_type=F32).astype(BF)
        if c == 0:
            pl.semaphore_wait(barrier, EXPERTS)
        for d in range(1, EXPERTS):
            ship(send, recv_a, ssem, rsem, c, d).start()
        recv_a[c, block(group), :] = send[c, block(group), :]

    def spread(src, c, at):
        x[at:at + rows, :] = src[c, :, :kc]
        wide = jnp.dot(unpack, src[c, :, kc:], preferred_element_type=F32).astype(BF)
        for k in range(8):
            x[at + rows:at + half, k * ow:(k + 1) * ow] = wide[k * ext:(k + 1) * ext]

    def forward(c):
        return pltpu.make_async_remote_copy(
            src_ref=recv_a.at[c], dst_ref=recv_b.at[c], send_sem=fs_sem.at[c],
            recv_sem=fr_sem.at[c], device_id=twin, device_id_type=MESH)

    for c in range(PARTS):
        for d in range(1, EXPERTS):
            landed(recv_a, ssem, rsem, c, d).wait_recv()
        forward(c).start()
        spread(recv_a, c, 0)
        for cp in in_copies(c):
            cp.wait()
        forward(c).wait_recv()
        spread(recv_b, c, half)

        def tile(t, carry):
            cols = pl.ds(pl.multiple_of(t * 2 * tw, 128), 2 * tw)
            both = jnp.dot(x[...], w_in[c, :, cols], preferred_element_type=F32)
            if c > 0:
                both = both + acc[:, cols]
            if c < PARTS - 1:
                acc[:, cols] = both
            else:
                g, u = both[:, :tw], both[:, tw:]
                hid[:, pl.ds(pl.multiple_of(t * tw, 128), tw)] = (
                    g / (1.0 + jnp.exp(-g)) * u).astype(BF)
            return carry

        lax.fori_loop(0, NT, tile, 0)

    def swap(n):
        return pltpu.make_async_remote_copy(
            src_ref=part_s.at[n], dst_ref=part_r.at[n], send_sem=ps_sem.at[n],
            recv_sem=pr_sem.at[n], device_id=twin, device_id_type=MESH)

    def finish(n):
        swap(n).wait_recv()
        total = (own[n % 2] + part_r[n].astype(F32)).astype(BF)
        rsend[n, :, :kc] = total[:rows]
        tall = jnp.concatenate(
            [total[rows:, k * ow:(k + 1) * ow] for k in range(8)], axis=0)
        rsend[n, :, kc:] = jnp.dot(pack, tall, preferred_element_type=F32).astype(BF)
        for d in range(1, EXPERTS):
            ship(rsend, ret, bs_sem, br_sem, n, d).start()
        ret[n, block(group), :] = rsend[n, block(group), :]

    for n in range(PARTS):
        out_copy(n).wait()

        def down(t, carry):
            cols = pl.ds(pl.multiple_of(t * 512, 512), 512)
            res = jnp.dot(hid[...], w_out[n % 2, :, cols], preferred_element_type=F32)
            own[n % 2, :, cols] = res[:half]
            part_s[n, :, cols] = res[half:].astype(BF)
            return carry

        lax.fori_loop(0, kc // 512, down, 0)
        swap(n).start()
        if n == 0:
            out_copy(2).start()
        if n > 0:
            finish(n - 1)
    finish(PARTS - 1)

    for n in range(PARTS):
        for d in range(1, EXPERTS):
            landed(ret, bs_sem, br_sem, n, d).wait_recv()
        base, extra = ret[n, :, :kc], ret[n, :, kc:]
        res = jnp.dot(gsc[0, 8 * n_tok:], base, preferred_element_type=F32)
        res = res + jnp.dot(gsc[1, 8 * n_tok:], base, preferred_element_type=F32)
        add = jnp.dot(gsc[0, :8 * n_tok], extra, preferred_element_type=F32)
        add = add + jnp.dot(gsc[1, :8 * n_tok], extra, preferred_element_type=F32)
        for k in range(8):
            out[:, n * kc + k * ow:n * kc + (k + 1) * ow] = (
                res[:, k * ow:(k + 1) * ow] + add[k * n_tok:(k + 1) * n_tok]).astype(BF)

    for c in range(PARTS):
        for d in range(1, EXPERTS):
            ship(send, recv_a, ssem, rsem, c, d).wait_send()
            ship(rsend, ret, bs_sem, br_sem, c, d).wait_send()
        forward(c).wait_send()
        swap(c).wait_send()


def local_pair(tokens, routes, gates, w_gate, w_up, w_down):
    n_tok, feat = tokens.shape
    ff = w_gate.shape[1]
    kc = feat // PARTS
    mw = kc + kc // 8
    rows = EXPERTS * BASE
    half = rows + EXPERTS * 2
    dma = pltpu.SemaphoreType.DMA
    vmem = pl.BlockSpec(memory_space=pltpu.VMEM)
    hbm = pl.BlockSpec(memory_space=pl.ANY)
    return pl.pallas_call(
        kernel,
        out_shape=jax.ShapeDtypeStruct((n_tok, feat), BF),
        in_specs=[vmem] * 3 + [hbm] * 3,
        out_specs=vmem,
        scratch_shapes=[
            pltpu.VMEM((PARTS, kc, 2 * ff), BF),
            pltpu.VMEM((2, ff, kc), BF),
            pltpu.VMEM((2 * half, 2 * ff), F32),
            pltpu.VMEM((2 * half, ff), BF),
            pltpu.VMEM((2 * half, kc), BF),
            pltpu.VMEM((PARTS, rows, mw), BF),
            pltpu.VMEM((PARTS, rows, mw), BF),
            pltpu.VMEM((PARTS, rows, mw), BF),
            pltpu.VMEM((2, half, kc), F32),
            pltpu.VMEM((PARTS, half, kc), BF),
            pltpu.VMEM((PARTS, half, kc), BF),
            pltpu.VMEM((PARTS, rows, mw), BF),
            pltpu.VMEM((PARTS, rows, mw), BF),
            pltpu.VMEM((2, 9 * n_tok, rows), BF),
            dma((PARTS, 2 * NT)),
            dma((2,)),
            dma((PARTS, EXPERTS)),
            dma((PARTS, EXPERTS)),
            dma((PARTS,)),
            dma((PARTS,)),
            dma((PARTS,)),
            dma((PARTS,)),
            dma((PARTS, EXPERTS)),
            dma((PARTS, EXPERTS)),
        ],
        compiler_params=pltpu.CompilerParams(
            collective_id=0, has_side_effects=True, vmem_limit_bytes=62 * 2**20),
    )(tokens, routes, gates, w_gate, w_up, w_down)


def solution(mesh):
    in_specs = (
        P(("parts", "tp"), None),
        P(("parts", "tp"), None),
        P(("parts", "tp"), None),
        P(None, "tp"),
        P(None, "tp"),
        P("tp", None),
    )
    out_specs = P(("parts", "tp"), None)
    local = local_pair if mesh.shape["tp"] == 2 * EXPERTS else local_any
    return jax.shard_map(local, mesh=mesh, in_specs=in_specs, out_specs=out_specs, check_vma=False)
```

```python
import functools

import jax
import jax.numpy as jnp
from jax import lax
from jax.experimental import pallas as pl
from jax.experimental.pallas import tpu as pltpu
from jax.sharding import PartitionSpec as P

EXPERTS = 8
TOP = 2
CAP = 18
BASE = 16
MESH = pl.DeviceIdType.MESH
BF = jnp.bfloat16
F32 = jnp.float32


def swapped(x, axis, bit):
    return lax.ppermute(x, axis, [(i, i ^ 1 << bit) for i in range(lax.axis_size(axis))])


def passed_along(value, axis, steps):
    count = lax.axis_size(axis)
    pairs = [(source, (source + steps) % count) for source in range(count)]
    return lax.ppermute(value, axis, pairs)


def expert_rows(chosen_rows, w_gate, w_up, w_down):
    gate_act = jnp.dot(chosen_rows, w_gate, preferred_element_type=jnp.float32)
    up_act = jnp.dot(chosen_rows, w_up, preferred_element_type=jnp.float32)
    hidden = (jax.nn.silu(gate_act) * up_act).astype(jnp.bfloat16)
    return jnp.dot(hidden, w_down, preferred_element_type=jnp.float32)


def local_any(tokens, routes, gates, w_gate, w_up, w_down):
    devices = lax.axis_size("tp")
    cycle_size = devices // EXPERTS
    levels = cycle_size.bit_length() - 1
    my_index = lax.axis_index("tp")
    my_group = my_index // cycle_size
    tok_count, feat_width = tokens.shape
    routed = routes.reshape(-1)
    pair_count = routed.shape[0]
    onehot = (routed[:, None] == jnp.arange(EXPERTS, dtype=jnp.int32)[None, :]).astype(jnp.int32)
    before = jnp.cumsum(onehot, axis=0) - onehot
    slot_index = jnp.sum(before * onehot, axis=1)
    target = routed * CAP + slot_index
    source_tok = jnp.arange(pair_count, dtype=jnp.int32) // TOP
    outgoing = (
        jnp.zeros((EXPERTS * CAP, feat_width), jnp.bfloat16).at[target].set(tokens[source_tok])
    )
    outgoing = outgoing.reshape(EXPERTS, CAP, feat_width)
    group_order = (my_group - jnp.arange(EXPERTS, dtype=jnp.int32)) % EXPERTS
    spread = jnp.repeat(outgoing, cycle_size, axis=0)
    incoming = lax.all_to_all(spread, "tp", split_axis=0, concat_axis=0, tiled=True)
    flat_rows = incoming.reshape(devices * CAP, feat_width)
    partial_value = expert_rows(flat_rows, w_gate, w_up, w_down)
    partial_value = partial_value.astype(jnp.bfloat16).reshape(devices, CAP, feat_width)
    current = lax.optimization_barrier(partial_value).astype(jnp.float32)
    current = current.reshape(EXPERTS, cycle_size, CAP, feat_width)
    for bit in range(levels):
        halves = current.reshape(EXPERTS, current.shape[1] // 2, 2, CAP, feat_width)
        upper = my_index // (1 << bit) % 2 == 1
        kept = jnp.where(upper, halves[:, :, 1], halves[:, :, 0])
        sending = jnp.where(upper, halves[:, :, 0], halves[:, :, 1])
        current = kept + swapped(sending.astype(jnp.bfloat16), "tp", bit).astype(sending.dtype)
    owned = current.reshape(EXPERTS, CAP, feat_width)
    back = [lax.dynamic_index_in_dim(owned, my_group, 0, keepdims=False)]
    for offset in range(1, EXPERTS):
        chosen = lax.dynamic_index_in_dim(owned, (my_group + offset) % EXPERTS, 0, keepdims=False)
        back.append(passed_along(chosen, "tp", offset * cycle_size))
    expert_out = jnp.take(jnp.stack(back), group_order, axis=0)
    picked = expert_out.reshape(EXPERTS * CAP, feat_width)[target]
    weighted = picked.reshape(tok_count, TOP, feat_width) * gates[:, :, None]
    return jnp.sum(weighted, axis=1).astype(jnp.bfloat16)


PARTS = 4
GROUPS = PARTS // 2
SLOTS = PARTS // 2 + 1
NT = 7


def iota(shape, dim):
    return lax.broadcasted_iota(jnp.int32, shape, dim)


def ones_where(mask, dtype=F32):
    return jnp.where(mask, 1.0, 0.0).astype(dtype)


def kernel(
    tok_hbm, routes, gates, wg, wu, wd, out,
    tok, w_in, w_out, acc, hid, x, send, recv_a, recv_b, own, part_s, part_r, wide, rsend, ret,
    gsc, res,
    tok_sem, in_sem, out_sem, ssem, rsem, fs_sem, fr_sem, ps_sem, pr_sem, bs_sem, br_sem,
):
    n_tok, feat = tok.shape
    kc = feat // PARTS
    ow = feat // 8
    ff = wg.shape[1]
    tw = ff // NT
    gr = feat // GROUPS
    rows = EXPERTS * BASE
    ext = EXPERTS * 2
    half = rows + ext
    me = lax.axis_index("tp")
    group = lax.div(me, 2)
    core = lax.rem(me, 2)
    twin = {"tp": group * 2 + (1 - core)}

    def peer(d):
        return lax.rem(group + d, EXPERTS)

    def in_copies(q):
        found = []
        for j in range(NT):
            for s, w in enumerate((wg, wu)):
                found.append(pltpu.make_async_copy(
                    w.at[pl.ds(q * gr, gr), pl.ds(j * tw, tw)],
                    w_in.at[pl.ds(q * gr, gr), pl.ds((2 * j + s) * tw, tw)],
                    in_sem.at[q, 2 * j + s]))
        return found

    def out_copy(n):
        return pltpu.make_async_copy(
            wd.at[:, pl.ds(n * kc, kc)], w_out.at[n % SLOTS], out_sem.at[n % SLOTS])

    def block(g):
        return pl.ds(pl.multiple_of(g * BASE, BASE), BASE)

    def there(c):
        return pl.ds(0, ow + kc) if c == 0 else pl.ds(ow + c * kc, kc)

    def home(n):
        return pl.ds(n * kc, kc + ow) if n == PARTS - 1 else pl.ds(n * kc, kc)

    barrier = pltpu.get_barrier_semaphore()
    for d in range(1, EXPERTS):
        pl.semaphore_signal(
            barrier, inc=1, device_id={"tp": peer(d) * 2 + core}, device_id_type=MESH)
    pl.semaphore_signal(barrier, inc=1, device_id=twin, device_id_type=MESH)
    fetch = pltpu.make_async_copy(tok_hbm, tok, tok_sem)
    fetch.start()

    def tiled(v):
        return jnp.concatenate([v] * 8, axis=1)

    line = iota((rows, n_tok), 0)
    named = ones_where((routes[0:1] == line >> 4) | (routes[1:2] == line >> 4), BF)
    wide_t = 8 * n_tok
    lane = iota((n_tok, wide_t), 1)
    earlier = ones_where(iota((n_tok, wide_t), 0) < lane & (n_tok - 1), BF)
    slot = jnp.dot(named, earlier, preferred_element_type=F32).astype(jnp.int32)
    line8 = iota((rows, wide_t), 0)
    lane8 = iota((rows, wide_t), 1)
    r8 = tiled(routes[...])
    first, second = r8[0:1] == line8 >> 4, r8[1:2] == line8 >> 4
    named8 = first | second
    over = named8 & (slot == BASE + ((line8 & 15) >> 3)) & (lane8 // n_tok == line8 & 7)
    main = named8 & (slot == line8 & 15)
    over_t = ones_where(over, BF)
    main_t = ones_where(main, BF)[:, :n_tok]

    def ship(src, dst, s_sem, r_sem, cols, c, d):
        to = peer(d)
        return pltpu.make_async_remote_copy(
            src_ref=src.at[block(to), cols], dst_ref=dst.at[block(group), cols],
            send_sem=s_sem.at[c, d], recv_sem=r_sem.at[c, group],
            device_id={"tp": to * 2 + core}, device_id_type=MESH)

    def landed(dst, s_sem, r_sem, cols, c, d):
        src = lax.rem(group + EXPERTS - d, EXPERTS)
        return pltpu.make_async_remote_copy(
            src_ref=dst.at[block(src), cols], dst_ref=dst.at[block(src), cols],
            send_sem=s_sem.at[c, d], recv_sem=r_sem.at[c, src],
            device_id=twin, device_id_type=MESH)

    def depart(c):
        for d in range(1, EXPERTS):
            ship(send, recv_a, ssem, rsem, there(c), c, d).start()

    fetch.wait()
    for c in range(PARTS):
        if c == 0:
            tall = jnp.concatenate([tok[:, k * ow:(k + 1) * ow] for k in range(8)], axis=0)
            send[:, :ow] = jnp.dot(over_t, tall, preferred_element_type=F32).astype(BF)
        send[:, ow + c * kc:ow + (c + 1) * kc] = jnp.dot(
            main_t, tok[:, c * kc:(c + 1) * kc], preferred_element_type=F32).astype(BF)
        if c == 0:
            pl.semaphore_wait(barrier, EXPERTS)
        if c < 2:
            depart(c)
        recv_a[block(group), there(c)] = send[block(group), there(c)]
        if c == 0:
            for cp in in_copies(0):
                cp.start()
    for q in range(1, GROUPS):
        for cp in in_copies(q):
            cp.start()
    for n in range(SLOTS):
        out_copy(n).start()

    g8 = tiled(gates[...])
    gate = jnp.where(first, g8[0:1], 0.0) + jnp.where(second, g8[1:2], 0.0)
    for at, size, full in (
        (0, wide_t, jnp.where(over, gate, 0.0)),
        (wide_t, n_tok, jnp.where(main, gate, 0.0)[:, :2 * n_tok]),
    ):
        full = full.T[:size]
        high = full.astype(BF)
        gsc[0, at:at + size] = high
        gsc[1, at:at + size] = (full - high.astype(F32)).astype(BF)

    i, j = iota((rows, rows), 0), iota((rows, rows), 1)
    unpack = ones_where(
        ((i >> 4) == (j & 7)) & (((i & 15) >> 1) == (j >> 4)) & ((i & 1) == ((j & 15) >> 3)), BF)
    pack = ones_where(
        ((j >> 4) == (i & 7)) & (((j & 15) >> 1) == (i >> 4)) & ((j & 1) == ((i & 15) >> 3)), BF)

    def spread(src, c, at):
        x[at:at + rows, c * kc:(c + 1) * kc] = src[:, ow + c * kc:ow + (c + 1) * kc]
        if c == 0:
            flat = jnp.dot(unpack, src[:, :ow], preferred_element_type=F32).astype(BF)
            for k in range(8):
                x[at + rows:at + half, k * ow:(k + 1) * ow] = flat[k * ext:(k + 1) * ext]

    def forward(c):
        return pltpu.make_async_remote_copy(
            src_ref=recv_a.at[:, there(c)], dst_ref=recv_b.at[:, there(c)],
            send_sem=fs_sem.at[c], recv_sem=fr_sem.at[c], device_id=twin, device_id_type=MESH)

    for c in range(PARTS):
        for d in range(1, EXPERTS):
            landed(recv_a, ssem, rsem, there(c), c, d).wait_recv()
        if c + 2 < PARTS:
            depart(c + 2)
        forward(c).start()
        spread(recv_a, c, 0)
        if c % (PARTS // GROUPS) == 0:
            for cp in in_copies(c // (PARTS // GROUPS)):
                cp.wait()
        forward(c).wait_recv()
        spread(recv_b, c, half)

        def tile(t, carry):
            cols = pl.ds(pl.multiple_of(t * 2 * tw, 128), 2 * tw)
            both = jnp.dot(
                x[:, c * kc:(c + 1) * kc], w_in[c * kc:(c + 1) * kc, cols],
                preferred_element_type=F32)
            if c > 0:
                both = both + acc[:, cols]
            if c < PARTS - 1:
                acc[:, cols] = both
            else:
                g, u = both[:, :tw], both[:, tw:]
                hid[:, pl.ds(pl.multiple_of(t * tw, 128), tw)] = (
                    g / (1.0 + jnp.exp(-g)) * u).astype(BF)
            return carry

        lax.fori_loop(0, NT, tile, 0)

    def swap(n):
        return pltpu.make_async_remote_copy(
            src_ref=part_s.at[n], dst_ref=part_r.at[n], send_sem=ps_sem.at[n],
            recv_sem=pr_sem.at[n], device_id=twin, device_id_type=MESH)

    def finish(n):
        swap(n).wait_recv()
        total = (own[n % 2] + part_r[n].astype(F32)).astype(BF)
        rsend[:, n * kc:(n + 1) * kc] = total[:rows]
        wide[:, n * kc:(n + 1) * kc] = total[rows:]
        if n == PARTS - 1:
            tall = jnp.concatenate([wide[:, k * ow:(k + 1) * ow] for k in range(8)], axis=0)
            rsend[:, feat:] = jnp.dot(pack, tall, preferred_element_type=F32).astype(BF)
        for d in range(1, EXPERTS):
            ship(rsend, ret, bs_sem, br_sem, home(n), n, d).start()
        ret[block(group), home(n)] = rsend[block(group), home(n)]

    for n in range(PARTS):
        out_copy(n).wait()
        down = jnp.dot(hid[...], w_out[n % SLOTS], preferred_element_type=F32)
        part_s[n] = down[half:].astype(BF)
        swap(n).start()
        own[n % 2] = down[:half]
        if n + SLOTS < PARTS:
            out_copy(n + SLOTS).start()
        if n > 0:
            finish(n - 1)
    finish(PARTS - 1)

    for n in range(PARTS):
        for d in range(1, EXPERTS):
            landed(ret, bs_sem, br_sem, home(n), n, d).wait_recv()
        base = ret[:, n * kc:(n + 1) * kc]
        here = jnp.dot(gsc[0, wide_t:], base, preferred_element_type=F32)
        res[:, n * kc:(n + 1) * kc] = here + jnp.dot(
            gsc[1, wide_t:], base, preferred_element_type=F32)
    extra = ret[:, feat:]
    add = jnp.dot(gsc[0, :wide_t], extra, preferred_element_type=F32)
    add = add + jnp.dot(gsc[1, :wide_t], extra, preferred_element_type=F32)
    for k in range(8):
        out[:, k * ow:(k + 1) * ow] = (
            res[:, k * ow:(k + 1) * ow] + add[k * n_tok:(k + 1) * n_tok]).astype(BF)

    for c in range(PARTS):
        for d in range(1, EXPERTS):
            ship(send, recv_a, ssem, rsem, there(c), c, d).wait_send()
            ship(rsend, ret, bs_sem, br_sem, home(c), c, d).wait_send()
        forward(c).wait_send()
        swap(c).wait_send()


def local_pair(tokens, routes, gates, w_gate, w_up, w_down):
    n_tok, feat = tokens.shape
    ff = w_gate.shape[1]
    kc = feat // PARTS
    mw = feat + feat // 8
    rows = EXPERTS * BASE
    half = rows + EXPERTS * 2
    dma = pltpu.SemaphoreType.DMA
    vmem = pl.BlockSpec(memory_space=pltpu.VMEM)
    hbm = pl.BlockSpec(memory_space=pl.ANY)
    return pl.pallas_call(
        kernel,
        out_shape=jax.ShapeDtypeStruct((n_tok, feat), BF),
        in_specs=[hbm] + [vmem] * 2 + [hbm] * 3,
        out_specs=vmem,
        scratch_shapes=[
            pltpu.VMEM((n_tok, feat), BF),
            pltpu.VMEM((feat, 2 * ff), BF),
            pltpu.VMEM((SLOTS, ff, kc), BF),
            pltpu.VMEM((2 * half, 2 * ff), F32),
            pltpu.VMEM((2 * half, ff), BF),
            pltpu.VMEM((2 * half, feat), BF),
            pltpu.VMEM((rows, mw), BF),
            pltpu.VMEM((rows, mw), BF),
            pltpu.VMEM((rows, mw), BF),
            pltpu.VMEM((2, half, kc), F32),
            pltpu.VMEM((PARTS, half, kc), BF),
            pltpu.VMEM((PARTS, half, kc), BF),
            pltpu.VMEM((EXPERTS * 2, feat), BF),
            pltpu.VMEM((rows, mw), BF),
            pltpu.VMEM((rows, mw), BF),
            pltpu.VMEM((2, 9 * n_tok, rows), BF),
            pltpu.VMEM((n_tok, feat), F32),
            dma,
            dma((GROUPS, 2 * NT)),
            dma((SLOTS,)),
            dma((PARTS, EXPERTS)),
            dma((PARTS, EXPERTS)),
            dma((PARTS,)),
            dma((PARTS,)),
            dma((PARTS,)),
            dma((PARTS,)),
            dma((PARTS, EXPERTS)),
            dma((PARTS, EXPERTS)),
        ],
        compiler_params=pltpu.CompilerParams(
            collective_id=0, has_side_effects=True, vmem_limit_bytes=63 * 2**20),
    )(tokens, routes.T, gates.T, w_gate, w_up, w_down)


def solution(mesh):
    in_specs = (
        P(("parts", "tp"), None),
        P(("parts", "tp"), None),
        P(("parts", "tp"), None),
        P(None, "tp"),
        P(None, "tp"),
        P("tp", None),
    )
    out_specs = P(("parts", "tp"), None)
    local = local_pair if mesh.shape["tp"] == 2 * EXPERTS else local_any
    return jax.shard_map(local, mesh=mesh, in_specs=in_specs, out_specs=out_specs, check_vma=False)
```

```python
import functools

import jax
import jax.numpy as jnp
from jax import lax
from jax.experimental import pallas as pl
from jax.experimental.pallas import tpu as pltpu
from jax.sharding import PartitionSpec as P

EXPERTS = 8
TOP = 2
CAP = 18
BASE = 16
MESH = pl.DeviceIdType.MESH
BF = jnp.bfloat16
F32 = jnp.float32


def swapped(x, axis, bit):
    return lax.ppermute(x, axis, [(i, i ^ 1 << bit) for i in range(lax.axis_size(axis))])


def passed_along(value, axis, steps):
    count = lax.axis_size(axis)
    pairs = [(source, (source + steps) % count) for source in range(count)]
    return lax.ppermute(value, axis, pairs)


def expert_rows(chosen_rows, w_gate, w_up, w_down):
    gate_act = jnp.dot(chosen_rows, w_gate, preferred_element_type=jnp.float32)
    up_act = jnp.dot(chosen_rows, w_up, preferred_element_type=jnp.float32)
    hidden = (jax.nn.silu(gate_act) * up_act).astype(jnp.bfloat16)
    return jnp.dot(hidden, w_down, preferred_element_type=jnp.float32)


def local_any(tokens, routes, gates, w_gate, w_up, w_down):
    devices = lax.axis_size("tp")
    cycle_size = devices // EXPERTS
    levels = cycle_size.bit_length() - 1
    my_index = lax.axis_index("tp")
    my_group = my_index // cycle_size
    tok_count, feat_width = tokens.shape
    routed = routes.reshape(-1)
    pair_count = routed.shape[0]
    onehot = (routed[:, None] == jnp.arange(EXPERTS, dtype=jnp.int32)[None, :]).astype(jnp.int32)
    before = jnp.cumsum(onehot, axis=0) - onehot
    slot_index = jnp.sum(before * onehot, axis=1)
    target = routed * CAP + slot_index
    source_tok = jnp.arange(pair_count, dtype=jnp.int32) // TOP
    outgoing = (
        jnp.zeros((EXPERTS * CAP, feat_width), jnp.bfloat16).at[target].set(tokens[source_tok])
    )
    outgoing = outgoing.reshape(EXPERTS, CAP, feat_width)
    group_order = (my_group - jnp.arange(EXPERTS, dtype=jnp.int32)) % EXPERTS
    spread = jnp.repeat(outgoing, cycle_size, axis=0)
    incoming = lax.all_to_all(spread, "tp", split_axis=0, concat_axis=0, tiled=True)
    flat_rows = incoming.reshape(devices * CAP, feat_width)
    partial_value = expert_rows(flat_rows, w_gate, w_up, w_down)
    partial_value = partial_value.astype(jnp.bfloat16).reshape(devices, CAP, feat_width)
    current = lax.optimization_barrier(partial_value).astype(jnp.float32)
    current = current.reshape(EXPERTS, cycle_size, CAP, feat_width)
    for bit in range(levels):
        halves = current.reshape(EXPERTS, current.shape[1] // 2, 2, CAP, feat_width)
        upper = my_index // (1 << bit) % 2 == 1
        kept = jnp.where(upper, halves[:, :, 1], halves[:, :, 0])
        sending = jnp.where(upper, halves[:, :, 0], halves[:, :, 1])
        current = kept + swapped(sending.astype(jnp.bfloat16), "tp", bit).astype(sending.dtype)
    owned = current.reshape(EXPERTS, CAP, feat_width)
    back = [lax.dynamic_index_in_dim(owned, my_group, 0, keepdims=False)]
    for offset in range(1, EXPERTS):
        chosen = lax.dynamic_index_in_dim(owned, (my_group + offset) % EXPERTS, 0, keepdims=False)
        back.append(passed_along(chosen, "tp", offset * cycle_size))
    expert_out = jnp.take(jnp.stack(back), group_order, axis=0)
    picked = expert_out.reshape(EXPERTS * CAP, feat_width)[target]
    weighted = picked.reshape(tok_count, TOP, feat_width) * gates[:, :, None]
    return jnp.sum(weighted, axis=1).astype(jnp.bfloat16)


PARTS = 4
GROUPS = PARTS // 2
SLOTS = PARTS // 2 + 1
NEAR = (1, 7, 2, 6, 3, 5, 4)
NT = 7


def iota(shape, dim):
    return lax.broadcasted_iota(jnp.int32, shape, dim)


def ones_where(mask, dtype=F32):
    return jnp.where(mask, 1.0, 0.0).astype(dtype)


def kernel(
    tok_hbm, routes, gates, wg, wu, wd, out,
    tok, w_in, w_out, acc, hid, x, send, recv_a, recv_b, own, part_s, part_r, wide, rsend, ret,
    gsc, res,
    tok_sem, in_sem, out_sem, ssem, rsem, fs_sem, fr_sem, ps_sem, pr_sem, bs_sem, br_sem,
):
    n_tok, feat = tok.shape
    kc = feat // PARTS
    ow = feat // 8
    ff = wg.shape[1]
    tw = ff // NT
    gr = feat // GROUPS
    rows = EXPERTS * BASE
    ext = EXPERTS * 2
    half = rows + ext
    me = lax.axis_index("tp")
    group = lax.div(me, 2)
    core = lax.rem(me, 2)
    twin = {"tp": group * 2 + (1 - core)}

    def peer(d):
        return lax.rem(group + NEAR[d - 1], EXPERTS)

    def in_copies(q):
        found = []
        for j in range(NT):
            for s, w in enumerate((wg, wu)):
                found.append(pltpu.make_async_copy(
                    w.at[pl.ds(q * gr, gr), pl.ds(j * tw, tw)],
                    w_in.at[pl.ds(q * gr, gr), pl.ds((2 * j + s) * tw, tw)],
                    in_sem.at[q, 2 * j + s]))
        return found

    def out_copy(n):
        return pltpu.make_async_copy(
            wd.at[:, pl.ds(n * kc, kc)], w_out.at[n % SLOTS], out_sem.at[n % SLOTS])

    def block(g):
        return pl.ds(pl.multiple_of(g * BASE, BASE), BASE)

    def there(c):
        return pl.ds(0, ow + kc) if c == 0 else pl.ds(ow + c * kc, kc)

    def home(n):
        return pl.ds(n * kc, kc + ow) if n == PARTS - 1 else pl.ds(n * kc, kc)

    barrier = pltpu.get_barrier_semaphore()
    for d in range(1, EXPERTS):
        pl.semaphore_signal(
            barrier, inc=1, device_id={"tp": peer(d) * 2 + core}, device_id_type=MESH)
    pl.semaphore_signal(barrier, inc=1, device_id=twin, device_id_type=MESH)
    fetch = pltpu.make_async_copy(tok_hbm, tok, tok_sem)
    fetch.start()

    def tiled(v):
        return jnp.concatenate([v] * 8, axis=1)

    line = iota((rows, n_tok), 0)
    named = ones_where((routes[0:1] == line >> 4) | (routes[1:2] == line >> 4), BF)
    wide_t = 8 * n_tok
    lane = iota((n_tok, wide_t), 1)
    earlier = ones_where(iota((n_tok, wide_t), 0) < lane & (n_tok - 1), BF)
    slot = jnp.dot(named, earlier, preferred_element_type=F32).astype(jnp.int32)
    line8 = iota((rows, wide_t), 0)
    lane8 = iota((rows, wide_t), 1)
    r8 = tiled(routes[...])
    first, second = r8[0:1] == line8 >> 4, r8[1:2] == line8 >> 4
    named8 = first | second
    over = named8 & (slot == BASE + ((line8 & 15) >> 3)) & (lane8 // n_tok == line8 & 7)
    main = named8 & (slot == line8 & 15)
    over_t = ones_where(over, BF)
    main_t = ones_where(main, BF)[:, :n_tok]

    def ship(src, dst, s_sem, r_sem, cols, c, d):
        to = peer(d)
        return pltpu.make_async_remote_copy(
            src_ref=src.at[block(to), cols], dst_ref=dst.at[block(group), cols],
            send_sem=s_sem.at[c, d], recv_sem=r_sem.at[c, group],
            device_id={"tp": to * 2 + core}, device_id_type=MESH)

    def landed(dst, s_sem, r_sem, cols, c, d):
        src = lax.rem(group + EXPERTS - NEAR[d - 1], EXPERTS)
        return pltpu.make_async_remote_copy(
            src_ref=dst.at[block(src), cols], dst_ref=dst.at[block(src), cols],
            send_sem=s_sem.at[c, d], recv_sem=r_sem.at[c, src],
            device_id=twin, device_id_type=MESH)

    def depart(c):
        for d in range(1, EXPERTS):
            ship(send, recv_a, ssem, rsem, there(c), c, d).start()

    fetch.wait()
    for c in range(PARTS):
        if c == 0:
            tall = jnp.concatenate([tok[:, k * ow:(k + 1) * ow] for k in range(8)], axis=0)
            send[:, :ow] = jnp.dot(over_t, tall, preferred_element_type=F32).astype(BF)
        send[:, ow + c * kc:ow + (c + 1) * kc] = jnp.dot(
            main_t, tok[:, c * kc:(c + 1) * kc], preferred_element_type=F32).astype(BF)
        if c == 0:
            pl.semaphore_wait(barrier, EXPERTS)
        if c < 2:
            depart(c)
        recv_a[block(group), there(c)] = send[block(group), there(c)]
        if c == 0:
            for cp in in_copies(0):
                cp.start()
    for q in range(1, GROUPS):
        for cp in in_copies(q):
            cp.start()
    for n in range(SLOTS):
        out_copy(n).start()

    g8 = tiled(gates[...])
    gate = jnp.where(first, g8[0:1], 0.0) + jnp.where(second, g8[1:2], 0.0)
    for at, size, full in (
        (0, wide_t, jnp.where(over, gate, 0.0)),
        (wide_t, n_tok, jnp.where(main, gate, 0.0)[:, :2 * n_tok]),
    ):
        full = full.T[:size]
        high = full.astype(BF)
        gsc[0, at:at + size] = high
        gsc[1, at:at + size] = (full - high.astype(F32)).astype(BF)

    i, j = iota((rows, rows), 0), iota((rows, rows), 1)
    unpack = ones_where(
        ((i >> 4) == (j & 7)) & (((i & 15) >> 1) == (j >> 4)) & ((i & 1) == ((j & 15) >> 3)), BF)
    pack = ones_where(
        ((j >> 4) == (i & 7)) & (((j & 15) >> 1) == (i >> 4)) & ((j & 1) == ((i & 15) >> 3)), BF)

    def spread(src, c, at):
        x[at:at + rows, c * kc:(c + 1) * kc] = src[:, ow + c * kc:ow + (c + 1) * kc]
        if c == 0:
            flat = jnp.dot(unpack, src[:, :ow], preferred_element_type=F32).astype(BF)
            for k in range(8):
                x[at + rows:at + half, k * ow:(k + 1) * ow] = flat[k * ext:(k + 1) * ext]

    def forward(c):
        return pltpu.make_async_remote_copy(
            src_ref=recv_a.at[:, there(c)], dst_ref=recv_b.at[:, there(c)],
            send_sem=fs_sem.at[c], recv_sem=fr_sem.at[c], device_id=twin, device_id_type=MESH)

    for c in range(PARTS):
        for d in range(1, EXPERTS):
            landed(recv_a, ssem, rsem, there(c), c, d).wait_recv()
        if c + 2 < PARTS:
            depart(c + 2)
        forward(c).start()
        spread(recv_a, c, 0)
        if c % (PARTS // GROUPS) == 0:
            for cp in in_copies(c // (PARTS // GROUPS)):
                cp.wait()
        forward(c).wait_recv()
        spread(recv_b, c, half)

        def tile(t, carry):
            cols = pl.ds(pl.multiple_of(t * 2 * tw, 128), 2 * tw)
            both = jnp.dot(
                x[:, c * kc:(c + 1) * kc], w_in[c * kc:(c + 1) * kc, cols],
                preferred_element_type=F32)
            if c > 0:
                both = both + acc[:, cols]
            if c < PARTS - 1:
                acc[:, cols] = both
            else:
                g, u = both[:, :tw], both[:, tw:]
                hid[:, pl.ds(pl.multiple_of(t * tw, 128), tw)] = (
                    g / (1.0 + jnp.exp(-g)) * u).astype(BF)
            return carry

        lax.fori_loop(0, NT, tile, 0)

    def swap(n):
        return pltpu.make_async_remote_copy(
            src_ref=part_s.at[n], dst_ref=part_r.at[n], send_sem=ps_sem.at[n],
            recv_sem=pr_sem.at[n], device_id=twin, device_id_type=MESH)

    def finish(n):
        swap(n).wait_recv()
        total = (own[n % 2] + part_r[n].astype(F32)).astype(BF)
        rsend[:, n * kc:(n + 1) * kc] = total[:rows]
        wide[:, n * kc:(n + 1) * kc] = total[rows:]
        if n == PARTS - 1:
            tall = jnp.concatenate([wide[:, k * ow:(k + 1) * ow] for k in range(8)], axis=0)
            rsend[:, feat:] = jnp.dot(pack, tall, preferred_element_type=F32).astype(BF)
        for d in range(1, EXPERTS):
            ship(rsend, ret, bs_sem, br_sem, home(n), n, d).start()
        ret[block(group), home(n)] = rsend[block(group), home(n)]

    for n in range(PARTS):
        out_copy(n).wait()
        down = jnp.dot(hid[...], w_out[n % SLOTS], preferred_element_type=F32)
        part_s[n] = down[half:].astype(BF)
        swap(n).start()
        own[n % 2] = down[:half]
        if n + SLOTS < PARTS:
            out_copy(n + SLOTS).start()
        if n > 0:
            finish(n - 1)
    finish(PARTS - 1)

    for n in range(PARTS):
        for d in range(1, EXPERTS):
            landed(ret, bs_sem, br_sem, home(n), n, d).wait_recv()
        base = ret[:, n * kc:(n + 1) * kc]
        here = jnp.dot(gsc[0, wide_t:], base, preferred_element_type=F32)
        res[:, n * kc:(n + 1) * kc] = here + jnp.dot(
            gsc[1, wide_t:], base, preferred_element_type=F32)
    extra = ret[:, feat:]
    add = jnp.dot(gsc[0, :wide_t], extra, preferred_element_type=F32)
    add = add + jnp.dot(gsc[1, :wide_t], extra, preferred_element_type=F32)
    for k in range(8):
        out[:, k * ow:(k + 1) * ow] = (
            res[:, k * ow:(k + 1) * ow] + add[k * n_tok:(k + 1) * n_tok]).astype(BF)

    for c in range(PARTS):
        for d in range(1, EXPERTS):
            ship(send, recv_a, ssem, rsem, there(c), c, d).wait_send()
            ship(rsend, ret, bs_sem, br_sem, home(c), c, d).wait_send()
        forward(c).wait_send()
        swap(c).wait_send()


def local_pair(tokens, routes, gates, w_gate, w_up, w_down):
    n_tok, feat = tokens.shape
    ff = w_gate.shape[1]
    kc = feat // PARTS
    mw = feat + feat // 8
    rows = EXPERTS * BASE
    half = rows + EXPERTS * 2
    dma = pltpu.SemaphoreType.DMA
    vmem = pl.BlockSpec(memory_space=pltpu.VMEM)
    hbm = pl.BlockSpec(memory_space=pl.ANY)
    return pl.pallas_call(
        kernel,
        out_shape=jax.ShapeDtypeStruct((n_tok, feat), BF),
        in_specs=[hbm] + [vmem] * 2 + [hbm] * 3,
        out_specs=vmem,
        scratch_shapes=[
            pltpu.VMEM((n_tok, feat), BF),
            pltpu.VMEM((feat, 2 * ff), BF),
            pltpu.VMEM((SLOTS, ff, kc), BF),
            pltpu.VMEM((2 * half, 2 * ff), F32),
            pltpu.VMEM((2 * half, ff), BF),
            pltpu.VMEM((2 * half, feat), BF),
            pltpu.VMEM((rows, mw), BF),
            pltpu.VMEM((rows, mw), BF),
            pltpu.VMEM((rows, mw), BF),
            pltpu.VMEM((2, half, kc), F32),
            pltpu.VMEM((PARTS, half, kc), BF),
            pltpu.VMEM((PARTS, half, kc), BF),
            pltpu.VMEM((EXPERTS * 2, feat), BF),
            pltpu.VMEM((rows, mw), BF),
            pltpu.VMEM((rows, mw), BF),
            pltpu.VMEM((2, 9 * n_tok, rows), BF),
            pltpu.VMEM((n_tok, feat), F32),
            dma,
            dma((GROUPS, 2 * NT)),
            dma((SLOTS,)),
            dma((PARTS, EXPERTS)),
            dma((PARTS, EXPERTS)),
            dma((PARTS,)),
            dma((PARTS,)),
            dma((PARTS,)),
            dma((PARTS,)),
            dma((PARTS, EXPERTS)),
            dma((PARTS, EXPERTS)),
        ],
        compiler_params=pltpu.CompilerParams(
            collective_id=0, has_side_effects=True, vmem_limit_bytes=63 * 2**20),
    )(tokens, routes.T, gates.T, w_gate, w_up, w_down)


def solution(mesh):
    in_specs = (
        P(("parts", "tp"), None),
        P(("parts", "tp"), None),
        P(("parts", "tp"), None),
        P(None, "tp"),
        P(None, "tp"),
        P("tp", None),
    )
    out_specs = P(("parts", "tp"), None)
    local = local_pair if mesh.shape["tp"] == 2 * EXPERTS else local_any
    return jax.shard_map(local, mesh=mesh, in_specs=in_specs, out_specs=out_specs, check_vma=False)
```
